32 devices in a mesh: dp: 8 (over z, x), fsdp: 4 (over y, core).
Axes of the slice: x: 2, y: 2, z: 4, core: 2. Of those that a mesh axis runs over, the one named last changes fastest.
Arguments:
- img_feat: bfloat16 [1536, 1536], P(('dp', 'fsdp')), may hold values from -6 to 6
- txt_feat: bfloat16 [1536, 1536], P(('dp', 'fsdp')), may hold values from -6 to 6
- img_weight: bfloat16 [1536, 1536], P('fsdp'), may hold values from -0.15625 to 0.15625
- txt_weight: bfloat16 [1536, 1536], P('fsdp'), may hold values from -0.15625 to 0.15625
- log_temp: float32 [1], replicated, may hold values from 1.5 to 2.5
- bias: float32 [1], replicated, may hold values from -6 to -4
Outputs:
- grad_img_weight: float32 [1536, 1536], P('fsdp')
- grad_txt_weight: float32 [1536, 1536], P('fsdp')
The draws below stay inside these ranges and needn't reach their ends.
All inputs are finite; a program needn't handle non-finite values.
Results may differ from the reference program's by a relative error of at most 0.0053.
Values may be sent and summed in bfloat16 or wider, within the bound.
A program may use at most 64 MiB of HBM per device.

```python
import jax
import jax.numpy as jnp
from jax import lax

WIDTH = 1536
EMBED = 1536
ROWS_DEV = 48
BATCH = 1536
N_FSDP = 4


def steps_of(own_key, dims, pieces, smallest, high):
    loudness, own = 1.0, jax.random.fold_in(own_key, 6)
    for dim, shards_of in pieces:
        steps = jnp.exp(jax.random.uniform(jax.random.fold_in(own, dim), (shards_of,), jnp.float32, smallest / len(pieces), high / len(pieces)))
        loudness = loudness * jnp.repeat(steps, dims[dim] // shards_of).reshape([-1 if axis == dim else 1 for axis in range(len(dims))])
    return loudness


def centred(rng, dims, spread, limit, shards=(), held_as=jnp.bfloat16):
    array = jax.random.normal(rng, dims, jnp.float32) * spread
    if len(shards) > 0:
        array = steps_of(rng, dims, shards, -0.22, 0.18) * array
    return jnp.clip(array, min=-limit, max=limit).astype(held_as)


def setup_inputs(seed: int = 0) -> dict:
    arg_keys = jax.random.split(jax.random.key(seed), 7)
    return {
        "img_feat": centred(arg_keys[0], (BATCH, WIDTH), 1.0, 6.0, ((0, 32),)),
        "txt_feat": centred(arg_keys[1], (BATCH, WIDTH), 1.0, 6.0, ((0, 32),)),
        "img_weight": centred(arg_keys[2], (WIDTH, EMBED), WIDTH ** -0.5, 0.15625, ((0, 4),)),
        "txt_weight": centred(arg_keys[3], (WIDTH, EMBED), WIDTH ** -0.5, 0.15625, ((0, 4),)),
        "log_temp": jnp.clip(jax.random.uniform(arg_keys[4], (1,), jnp.float32, 1.5, 2.5), 1.5, 2.5),
        "bias": jnp.clip(jax.random.uniform(arg_keys[5], (1,), jnp.float32, -6.0, -4.0), -6.0, -4.0),
    }


EPS = 1e-06

def factor(y_rows):
    mean_sq = lax.optimization_barrier(jnp.mean(y_rows * y_rows, -1, keepdims=True))
    return (lax.rsqrt(mean_sq + EPS) * y_rows.shape[-1] ** (-0.5), mean_sq)

def back_norm(y_rows, grad_rows):
    norm_factor, mean_sq = factor(y_rows)
    inner_sum = lax.optimization_barrier(jnp.sum(y_rows * grad_rows, -1, keepdims=True))
    result = norm_factor * grad_rows - norm_factor * y_rows * inner_sum / (y_rows.shape[-1] * (mean_sq + EPS))
    return result.astype(jnp.bfloat16)

def reference(img_feat, txt_feat, img_weight, txt_weight, log_temp, bias):
    y_img = jnp.dot(img_feat, img_weight, preferred_element_type=jnp.float32)
    y_txt = jnp.dot(txt_feat, txt_weight, preferred_element_type=jnp.float32)
    img_factor, unused_img = factor(y_img)
    txt_factor, unused_txt = factor(y_txt)
    z_img = (y_img * img_factor).astype(jnp.bfloat16)
    z_txt = (y_txt * txt_factor).astype(jnp.bfloat16)
    temp_scale = jnp.exp(log_temp[0])
    bias_value = bias[0]
    block_rows = ROWS_DEV * N_FSDP
    block_total = BATCH // block_rows
    col_ids = jnp.arange(BATCH, dtype=jnp.int32)

    def block_step(grad_txt, block_item):
        img_rows, first_row = block_item
        logits = temp_scale * lax.dot_general(img_rows, z_txt, (((1,), (1,)), ((), ())), preferred_element_type=jnp.float32) + bias_value
        row_ids = first_row + jnp.arange(block_rows, dtype=jnp.int32)
        pair_label = jnp.where(row_ids[:, None] == col_ids[None, :], 1.0, -1.0).astype(jnp.float32)
        pair_weight = (temp_scale * (-pair_label * jax.nn.sigmoid(-pair_label * logits))).astype(jnp.bfloat16)
        grad_img_rows = jnp.dot(pair_weight, z_txt, preferred_element_type=jnp.float32)
        grad_txt = grad_txt + lax.dot_general(pair_weight, img_rows, (((0,), (0,)), ((), ())), preferred_element_type=jnp.float32)
        return (grad_txt, grad_img_rows)
    block_items = (z_img.reshape(block_total, block_rows, EMBED), jnp.arange(block_total, dtype=jnp.int32) * block_rows)
    grad_txt, grad_img = lax.scan(block_step, jnp.zeros((BATCH, EMBED), jnp.float32), block_items)
    grad_img = grad_img.reshape(BATCH, EMBED)
    dy_img = back_norm(y_img, grad_img)
    dy_txt = back_norm(y_txt, grad_txt)
    grad_img_weight = jnp.dot(img_feat.T, dy_img, preferred_element_type=jnp.float32)
    grad_txt_weight = jnp.dot(txt_feat.T, dy_txt, preferred_element_type=jnp.float32)
    return (grad_img_weight, grad_txt_weight)
```

```python
import functools

import jax
import jax.numpy as jnp
from jax import lax
from jax.experimental import pallas as pl
from jax.experimental.pallas import tpu as pltpu
from jax.sharding import PartitionSpec as P

EPS = 1e-06


def factor(y_rows):
    mean_sq = jnp.mean(y_rows * y_rows, -1, keepdims=True)
    return (lax.rsqrt(mean_sq + EPS) * y_rows.shape[-1] ** (-0.5), mean_sq)


def back_norm(y_rows, grad_rows):
    norm_factor, mean_sq = factor(y_rows)
    inner_sum = jnp.sum(y_rows * grad_rows, -1, keepdims=True)
    result = norm_factor * grad_rows - norm_factor * y_rows * inner_sum / (
        y_rows.shape[-1] * (mean_sq + EPS)
    )
    return result.astype(jnp.bfloat16)


def by_collectives(img_feat, txt_feat, img_weight, txt_weight, log_temp, bias):
    row_count = img_feat.shape[0]
    groups = lax.axis_size("fsdp")
    dp_index = lax.axis_index("dp")
    fsdp_index = lax.axis_index("fsdp")
    img_cols, txt_cols = (
        lax.all_to_all(img_feat, "fsdp", split_axis=1, concat_axis=0, tiled=True),
        lax.all_to_all(txt_feat, "fsdp", split_axis=1, concat_axis=0, tiled=True),
    )
    y_img = jnp.dot(
        img_feat,
        lax.all_gather(img_weight, "fsdp", axis=0, tiled=True),
        preferred_element_type=jnp.float32,
    )
    y_txt = jnp.dot(
        txt_feat,
        lax.all_gather(txt_weight, "fsdp", axis=0, tiled=True),
        preferred_element_type=jnp.float32,
    )
    img_factor, unused_img = factor(y_img)
    z_own = (y_img * img_factor).astype(jnp.bfloat16)
    image_block = lax.all_gather(z_own, "fsdp", axis=0, tiled=True)
    txt_factor, unused_txt = factor(y_txt)
    z_txt = (y_txt * txt_factor).astype(jnp.bfloat16)
    temp_scale = jnp.exp(log_temp[0])
    bias_value = bias[0]
    group_rows = image_block.shape[0]
    image_ids = dp_index * groups * row_count + jnp.arange(group_rows, dtype=jnp.int32)
    text_piece = lax.all_gather(z_txt, "dp", axis=0, tiled=True)
    length = text_piece.shape[0]
    text_pos = jnp.arange(length, dtype=jnp.int32)
    text_ids = (text_pos // row_count * groups + fsdp_index) * row_count + text_pos % row_count
    logits = (
        temp_scale
        * lax.dot_general(
            image_block, text_piece, (((1,), (1,)), ((), ())), preferred_element_type=jnp.float32
        )
        + bias_value
    )
    pair_label = jnp.where(image_ids[:, None] == text_ids[None, :], 1.0, -1.0).astype(jnp.float32)
    pair_weight = (temp_scale * (-pair_label * jax.nn.sigmoid(-pair_label * logits))).astype(
        jnp.bfloat16
    )
    grad_sum = jnp.dot(pair_weight, text_piece, preferred_element_type=jnp.float32)
    grad_txt = lax.psum_scatter(
        lax.dot_general(
            pair_weight, image_block, (((0,), (0,)), ((), ())), preferred_element_type=jnp.float32
        ),
        "dp",
        scatter_dimension=0,
        tiled=True,
    )
    grad_img = lax.psum_scatter(grad_sum, "fsdp", scatter_dimension=0, tiled=True)
    dy_img = back_norm(y_img, grad_img)
    dy_txt = back_norm(y_txt, grad_txt)
    dy_img_group, dy_txt_group = (
        lax.all_gather(dy_img, "fsdp", axis=0, tiled=True),
        lax.all_gather(dy_txt, "fsdp", axis=0, tiled=True),
    )
    weight_img = lax.dot_general(
        img_cols, dy_img_group, (((0,), (0,)), ((), ())), preferred_element_type=jnp.float32
    )
    weight_txt = lax.dot_general(
        txt_cols, dy_txt_group, (((0,), (0,)), ((), ())), preferred_element_type=jnp.float32
    )
    grad_img_weight, grad_txt_weight = lax.psum((weight_img, weight_txt), "dp")
    return (grad_img_weight, grad_txt_weight)


BF16 = jnp.bfloat16
F32 = jnp.float32
SIDE = 2


def dot(a, b, a_dim, b_dim):
    return lax.dot_general(a, b, (((a_dim,), (b_dim,)), ((), ())), preferred_element_type=F32)


def kernel(
    dims, img, txt, w_img, w_txt, log_temp, bias, out,
    cols, feats, part, part16, part_in, y_keep, z_img, z_txt,
    d_img, d_img16, d_img_in, d_txt, d_txt16, d_txt_in, dy, dy_all,
    send_sem, recv_sem,
):
    dp_n, groups, rows, width, embed = dims
    depth_n = dp_n // SIDE
    plane_n = SIDE * groups
    wide, tall = width // groups, embed // depth_n
    me_dp, me_f = lax.axis_index("dp"), lax.axis_index("fsdp")
    depth, side = me_dp // SIDE, me_dp % SIDE
    spot = side * groups + me_f
    count = [0]

    def send(source, target, to_dp, to_f):
        number = count[0]
        count[0] += 1
        copy = pltpu.make_async_remote_copy(
            src_ref=source, dst_ref=target,
            send_sem=send_sem.at[number], recv_sem=recv_sem.at[number],
            device_id=(to_dp, to_f), device_id_type=pl.DeviceIdType.MESH,
        )
        copy.start()
        sent.append(copy)
        return copy

    sent = []

    def at_spot(k):
        other = (spot + k) % plane_n
        return depth * SIDE + other // groups, other % groups

    def at_depth(k):
        return (depth + k) % depth_n

    def lanes(start, size):
        return pl.ds(pl.multiple_of(start * size, size), size)

    barrier = pltpu.get_barrier_semaphore()
    peers = [at_spot(k) for k in range(1, plane_n)]
    peers += [
        (at_depth(k) * SIDE + s, me_f) for k in range(1, depth_n) for s in range(SIDE)
    ]
    for peer in peers:
        pl.semaphore_signal(barrier, inc=1, device_id=peer, device_id_type=pl.DeviceIdType.MESH)
    pl.semaphore_wait(barrier, len(peers))

    got_cols = []
    for tower, feat in ((1, txt), (0, img)):
        for k in range(1, groups):
            to_f = (me_f + k) % groups
            got_cols.append(
                send(feat.at[:, lanes(to_f, wide)], cols.at[tower, me_f], me_dp, to_f)
            )
    for tower, feat in ((1, txt), (0, img)):
        cols[tower, me_f] = feat[:, lanes(me_f, wide)]

    tile = 384 if embed % 384 == 0 else 128
    got_part = {}
    for tower, weight in ((1, w_txt), (0, w_img)):
        for k in range(1, groups):
            got_cols.pop(0).wait_recv()

        def y_tile(j, carry, tower=tower, weight=weight):
            where = lanes(j, tile)
            term = dot(cols[tower].reshape(groups * rows, wide), weight[:, where], 1, 0)
            term = term.reshape(groups, rows, tile)
            part[tower, :, :, where] = term
            part16[tower, :, :, where] = term.astype(BF16)
            return carry

        lax.fori_loop(0, embed // tile, y_tile, 0)
        got_part[tower] = [
            send(part16.at[tower, (me_f + k) % groups], part_in.at[tower, k - 1],
                 me_dp, (me_f + k) % groups)
            for k in range(1, groups)
        ]

    feats[me_dp] = cols[side]
    got_feats = []
    for k in range(1, dp_n):
        to_dp = (me_dp + k) % dp_n
        got_feats.append(send(cols.at[to_dp % SIDE], feats.at[me_dp], to_dp, me_f))

    def y_rows(tower):
        for copy in got_part[tower]:
            copy.wait_recv()
        total = part[tower, me_f]
        for k in range(1, groups):
            total = total + part_in[tower, k - 1].astype(F32)
        y_keep[tower] = total
        norm_factor, _ = factor(total)
        return (total * norm_factor).astype(BF16)

    z_txt[depth] = y_rows(1)
    got_txt = [
        send(z_txt.at[depth], z_txt.at[depth], at_depth(k) * SIDE + side, me_f)
        for k in range(1, depth_n)
    ]
    z_img[spot] = y_rows(0)
    got_img = [
        send(z_img.at[spot], z_img.at[spot], *at_spot(k)) for k in range(1, plane_n)
    ]
    for copy in got_txt + got_img:
        copy.wait_recv()

    n_img, n_txt = plane_n * rows, depth_n * rows
    scale = jnp.exp(jnp.full((1, n_txt), log_temp[0], F32))
    scores = dot(
        z_img[...].reshape(n_img, embed), z_txt[...].reshape(n_txt, embed), 1, 1
    )
    scores = scale * scores + bias[0]
    row = lax.broadcasted_iota(jnp.int32, (n_img, n_txt), 0) - spot * rows
    col = lax.broadcasted_iota(jnp.int32, (n_img, n_txt), 1) - depth * rows
    label = jnp.where((row == col) & (row >= 0) & (row < rows), 1.0, -1.0).astype(F32)
    pair = (scale * (-label * jax.nn.sigmoid(-label * scores))).astype(BF16)

    def txt_tile(j, carry):
        where = lanes(j, tile)
        term = dot(pair, z_img[:, :, where].reshape(n_img, tile), 0, 0)
        term = term.reshape(depth_n, rows, tile)
        d_txt[:, :, where] = term
        d_txt16[:, :, where] = term.astype(BF16)
        return carry

    lax.fori_loop(0, embed // tile, txt_tile, 0)
    got_txt = [
        send(d_txt16.at[at_depth(k)], d_txt_in.at[k - 1], at_depth(k) * SIDE + side, me_f)
        for k in range(1, depth_n)
    ]

    def img_tile(j, carry):
        where = lanes(j, tile)
        term = dot(pair, z_txt[:, :, where].reshape(n_txt, tile), 1, 0)
        term = term.reshape(plane_n, rows, tile)
        d_img[:, :, where] = term
        d_img16[:, :, where] = term.astype(BF16)
        return carry

    lax.fori_loop(0, embed // tile, img_tile, 0)
    got_img = [
        send(d_img16.at[(spot + k) % plane_n], d_img_in.at[k - 1], *at_spot(k))
        for k in range(1, plane_n)
    ]

    for tower, copies, own, arrived in (
        (1, got_txt, d_txt[depth], d_txt_in),
        (0, got_img, d_img[spot], d_img_in),
    ):
        for k, copy in enumerate(copies):
            copy.wait_recv()
            own = own + arrived[k].astype(F32)
        dy[tower] = back_norm(y_keep[tower], own)

    got_dy = []
    for k in range(1, dp_n):
        to_dp = (me_dp + k) % dp_n
        got_dy.append(
            send(dy.at[to_dp % SIDE, :, lanes(to_dp // SIDE, tall)], dy_all.at[me_f, me_dp],
                 to_dp, me_f)
        )
    dy_all[me_f, me_dp] = dy[side, :, lanes(depth, tall)]
    for copy in got_dy + got_feats:
        copy.wait_recv()
    half = groups // 2
    across = (me_f + half) % groups
    twin = me_f + 1 - 2 * (me_f % 2)
    from_across = send(dy_all.at[me_f], dy_all.at[me_f], me_dp, across)
    from_twin = send(dy_all.at[me_f], dy_all.at[me_f], me_dp, twin)

    def grad_of(group):
        left = feats[:, group].reshape(dp_n * rows, wide)
        return dot(left, dy_all[group].reshape(dp_n * rows, tall), 0, 0)

    grad = grad_of(me_f)
    from_twin.wait_recv()
    grad = grad + grad_of(twin)
    from_across.wait_recv()
    passed_on = send(dy_all.at[across], dy_all.at[across], me_dp, twin)
    grad = grad + grad_of(across)
    passed_on.wait_recv()
    grad = grad + grad_of((twin + half) % groups)
    out[side, depth] = grad.astype(BF16)

    beside = depth * SIDE + (1 - side)
    along = [
        send(out.at[side, depth], out.at[side, depth], at_depth(k) * SIDE + side, me_f)
        for k in range(1, depth_n)
    ]
    over = [send(out.at[side, depth], out.at[side, depth], beside, me_f)]
    for k in range(1, depth_n):
        along[k - 1].wait_recv()
        place = (depth + depth_n - k) % depth_n
        over.append(send(out.at[side, place], out.at[side, place], beside, me_f))
    for copy in over:
        copy.wait_recv()
    for copy in sent:
        copy.wait_send()


def in_one_kernel(dp_n, groups, img_feat, txt_feat, img_weight, txt_weight, log_temp, bias):
    rows, width = img_feat.shape
    wide, embed = img_weight.shape
    depth_n, plane_n = dp_n // SIDE, SIDE * groups
    tall = embed // depth_n
    copies = 2 * 2 * (groups - 1) + 2 * (dp_n - 1) + 3 + 2 * (depth_n - 1 + plane_n - 1)
    copies += 2 * depth_n - 1
    vmem = pl.BlockSpec(memory_space=pltpu.VMEM)
    smem = pl.BlockSpec(memory_space=pltpu.SMEM)
    tiles = pl.pallas_call(
        functools.partial(kernel, (dp_n, groups, rows, width, embed)),
        out_shape=jax.ShapeDtypeStruct((SIDE, depth_n, wide, tall), BF16),
        in_specs=[vmem] * 4 + [smem] * 2,
        out_specs=vmem,
        scratch_shapes=[
            pltpu.VMEM((2, groups, rows, wide), BF16),
            pltpu.VMEM((dp_n, groups, rows, wide), BF16),
            pltpu.VMEM((2, groups, rows, embed), F32),
            pltpu.VMEM((2, groups, rows, embed), BF16),
            pltpu.VMEM((2, groups - 1, rows, embed), BF16),
            pltpu.VMEM((2, rows, embed), F32),
            pltpu.VMEM((plane_n, rows, embed), BF16),
            pltpu.VMEM((depth_n, rows, embed), BF16),
            pltpu.VMEM((plane_n, rows, embed), F32),
            pltpu.VMEM((plane_n, rows, embed), BF16),
            pltpu.VMEM((plane_n - 1, rows, embed), BF16),
            pltpu.VMEM((depth_n, rows, embed), F32),
            pltpu.VMEM((depth_n, rows, embed), BF16),
            pltpu.VMEM((depth_n - 1, rows, embed), BF16),
            pltpu.VMEM((2, rows, embed), BF16),
            pltpu.VMEM((groups, dp_n, rows, tall), BF16),
            pltpu.SemaphoreType.DMA((copies,)),
            pltpu.SemaphoreType.DMA((copies,)),
        ],
        compiler_params=pltpu.CompilerParams(
            collective_id=0, has_side_effects=True, vmem_limit_bytes=48 * 2**20
        ),
    )(img_feat, txt_feat, img_weight, txt_weight, log_temp, bias)
    whole = tiles.transpose(0, 2, 1, 3).reshape(SIDE, wide, embed).astype(F32)
    return (whole[0], whole[1])


def on_device(dp_n, groups, img_feat, txt_feat, img_weight, txt_weight, log_temp, bias):
    arrays = (img_feat, txt_feat, img_weight, txt_weight, log_temp, bias)
    rows = img_feat.shape[0]
    wide, embed = img_weight.shape
    depth_n = dp_n // SIDE
    held = embed * rows * (12 * SIDE * groups + 10 * depth_n + 28 * groups)
    held += 2 * rows * dp_n * groups * (wide + embed // depth_n) + 12 * wide * embed
    if (
        dp_n % SIDE or groups != 4 or rows % 16 or wide % 128
        or embed % (128 * depth_n) or held > 40 * 2**20
    ):
        return by_collectives(*arrays)
    return in_one_kernel(dp_n, groups, *arrays)


def solution(mesh):
    placed = (
        P(("dp", "fsdp"), None),
        P(("dp", "fsdp"), None),
        P("fsdp", None),
        P("fsdp", None),
        P(),
        P(),
    )
    return jax.shard_map(
        functools.partial(on_device, mesh.shape["dp"], mesh.shape["fsdp"]),
        mesh=mesh,
        in_specs=placed,
        out_specs=(P("fsdp", None), P("fsdp", None)),
        check_vma=False,
    )
```

```python
import functools

import jax
import jax.numpy as jnp
from jax import lax
from jax.experimental import pallas as pl
from jax.experimental.pallas import tpu as pltpu
from jax.sharding import PartitionSpec as P

EPS = 1e-06


def factor(y_rows):
    mean_sq = jnp.mean(y_rows * y_rows, -1, keepdims=True)
    return (lax.rsqrt(mean_sq + EPS) * y_rows.shape[-1] ** (-0.5), mean_sq)


def back_norm(y_rows, grad_rows):
    norm_factor, mean_sq = factor(y_rows)
    inner_sum = jnp.sum(y_rows * grad_rows, -1, keepdims=True)
    result = norm_factor * grad_rows - norm_factor * y_rows * inner_sum / (
        y_rows.shape[-1] * (mean_sq + EPS)
    )
    return result.astype(jnp.bfloat16)


def by_collectives(img_feat, txt_feat, img_weight, txt_weight, log_temp, bias):
    row_count = img_feat.shape[0]
    groups = lax.axis_size("fsdp")
    dp_index = lax.axis_index("dp")
    fsdp_index = lax.axis_index("fsdp")
    img_cols, txt_cols = (
        lax.all_to_all(img_feat, "fsdp", split_axis=1, concat_axis=0, tiled=True),
        lax.all_to_all(txt_feat, "fsdp", split_axis=1, concat_axis=0, tiled=True),
    )
    y_img = jnp.dot(
        img_feat,
        lax.all_gather(img_weight, "fsdp", axis=0, tiled=True),
        preferred_element_type=jnp.float32,
    )
    y_txt = jnp.dot(
        txt_feat,
        lax.all_gather(txt_weight, "fsdp", axis=0, tiled=True),
        preferred_element_type=jnp.float32,
    )
    img_factor, unused_img = factor(y_img)
    z_own = (y_img * img_factor).astype(jnp.bfloat16)
    image_block = lax.all_gather(z_own, "fsdp", axis=0, tiled=True)
    txt_factor, unused_txt = factor(y_txt)
    z_txt = (y_txt * txt_factor).astype(jnp.bfloat16)
    temp_scale = jnp.exp(log_temp[0])
    bias_value = bias[0]
    group_rows = image_block.shape[0]
    image_ids = dp_index * groups * row_count + jnp.arange(group_rows, dtype=jnp.int32)
    text_piece = lax.all_gather(z_txt, "dp", axis=0, tiled=True)
    length = text_piece.shape[0]
    text_pos = jnp.arange(length, dtype=jnp.int32)
    text_ids = (text_pos // row_count * groups + fsdp_index) * row_count + text_pos % row_count
    logits = (
        temp_scale
        * lax.dot_general(
            image_block, text_piece, (((1,), (1,)), ((), ())), preferred_element_type=jnp.float32
        )
        + bias_value
    )
    pair_label = jnp.where(image_ids[:, None] == text_ids[None, :], 1.0, -1.0).astype(jnp.float32)
    pair_weight = (temp_scale * (-pair_label * jax.nn.sigmoid(-pair_label * logits))).astype(
        jnp.bfloat16
    )
    grad_sum = jnp.dot(pair_weight, text_piece, preferred_element_type=jnp.float32)
    grad_txt = lax.psum_scatter(
        lax.dot_general(
            pair_weight, image_block, (((0,), (0,)), ((), ())), preferred_element_type=jnp.float32
        ),
        "dp",
        scatter_dimension=0,
        tiled=True,
    )
    grad_img = lax.psum_scatter(grad_sum, "fsdp", scatter_dimension=0, tiled=True)
    dy_img = back_norm(y_img, grad_img)
    dy_txt = back_norm(y_txt, grad_txt)
    dy_img_group, dy_txt_group = (
        lax.all_gather(dy_img, "fsdp", axis=0, tiled=True),
        lax.all_gather(dy_txt, "fsdp", axis=0, tiled=True),
    )
    weight_img = lax.dot_general(
        img_cols, dy_img_group, (((0,), (0,)), ((), ())), preferred_element_type=jnp.float32
    )
    weight_txt = lax.dot_general(
        txt_cols, dy_txt_group, (((0,), (0,)), ((), ())), preferred_element_type=jnp.float32
    )
    grad_img_weight, grad_txt_weight = lax.psum((weight_img, weight_txt), "dp")
    return (grad_img_weight, grad_txt_weight)


BF16 = jnp.bfloat16
F32 = jnp.float32
SIDE = 2


def dot(a, b, a_dim, b_dim):
    return lax.dot_general(a, b, (((a_dim,), (b_dim,)), ((), ())), preferred_element_type=F32)


def kernel(
    dims, img, txt, w_img_hbm, w_txt_hbm, log_temp, bias, out,
    w_img, w_txt, cols, feats, part, part16, part_in, y_keep, z_img, z_txt,
    d_img, d_img16, d_img_in, d_txt, d_txt16, d_txt_in, dy, dy_all,
    send_sem, recv_sem, local_sem, line_send, line_recv, over_send, over_recv,
):
    dp_n, groups, rows, width, embed = dims
    depth_n = dp_n // SIDE
    plane_n = SIDE * groups
    wide, tall = width // groups, embed // depth_n
    me_dp, me_f = lax.axis_index("dp"), lax.axis_index("fsdp")
    depth, side = me_dp // SIDE, me_dp % SIDE
    spot = side * groups + me_f
    count = [0]

    def send(source, target, to_dp, to_f):
        number = count[0]
        count[0] += 1
        copy = pltpu.make_async_remote_copy(
            src_ref=source, dst_ref=target,
            send_sem=send_sem.at[number], recv_sem=recv_sem.at[number],
            device_id=(to_dp, to_f), device_id_type=pl.DeviceIdType.MESH,
        )
        copy.start()
        sent.append(copy)
        return copy

    sent = []

    def at_spot(k):
        other = (spot + k) % plane_n
        return depth * SIDE + other // groups, other % groups

    def at_depth(k):
        return (depth + k) % depth_n

    def lanes(start, size):
        return pl.ds(pl.multiple_of(start * size, size), size)

    def line_hop(use, view, way, step):
        place, to = depth + way * step, depth - way
        return pltpu.make_async_remote_copy(
            src_ref=view(place), dst_ref=view(place),
            send_sem=line_send.at[use, (way + 1) // 2, step],
            recv_sem=line_recv.at[use, (way + 1) // 2, step],
            device_id=(to * SIDE + side, me_f), device_id_type=pl.DeviceIdType.MESH,
        )

    def on_line(place):
        return (place >= 0) & (place < depth_n)

    def line_step(use, view, step, then=None):
        for way in (-1, 1):
            place, to = depth + way * step, depth - way

            if step > 0:
                @pl.when(on_line(place))
                def _(way=way):
                    line_hop(use, view, way, step - 1).wait_recv()

            if step < depth_n - 1:
                @pl.when(on_line(place) & on_line(to))
                def _(way=way):
                    line_hop(use, view, way, step).start()

            if then is not None and (step > 0 or way > 0):
                @pl.when(on_line(place))
                def _(way=way, place=place):
                    then(way, step, place)

    def line_sent(use, view):
        for step in range(depth_n - 1):
            for way in (-1, 1):
                @pl.when(on_line(depth + way * step) & on_line(depth - way))
                def _(way=way, step=step):
                    line_hop(use, view, way, step).wait_send()

    own_copies = [
        pltpu.make_async_copy(img.at[:, lanes(me_f, wide)], cols.at[0, me_f], local_sem.at[0]),
        pltpu.make_async_copy(txt.at[:, lanes(me_f, wide)], cols.at[1, me_f], local_sem.at[1]),
        pltpu.make_async_copy(w_img_hbm, w_img, local_sem.at[2]),
        pltpu.make_async_copy(w_txt_hbm, w_txt, local_sem.at[3]),
    ]
    for copy in own_copies:
        copy.start()

    barrier = pltpu.get_barrier_semaphore()
    peers = [at_spot(k) for k in range(1, plane_n)]
    peers += [
        (at_depth(k) * SIDE + s, me_f) for k in range(1, depth_n) for s in range(SIDE)
    ]
    for peer in peers:
        pl.semaphore_signal(barrier, inc=1, device_id=peer, device_id_type=pl.DeviceIdType.MESH)
    pl.semaphore_wait(barrier, len(peers))

    got_cols = []
    for tower, feat in ((1, txt), (0, img)):
        for k in range(1, groups):
            to_f = (me_f + k) % groups
            got_cols.append(
                send(feat.at[:, lanes(to_f, wide)], cols.at[tower, me_f], me_dp, to_f)
            )
    for copy in own_copies:
        copy.wait()

    tile = 384 if embed % 384 == 0 else 128
    got_part = {}
    for tower, weight in ((1, w_txt), (0, w_img)):
        for k in range(1, groups):
            got_cols.pop(0).wait_recv()

        def y_tile(j, carry, tower=tower, weight=weight):
            where = lanes(j, tile)
            term = dot(cols[tower].reshape(groups * rows, wide), weight[:, where], 1, 0)
            term = term.reshape(groups, rows, tile)
            part[tower, :, :, where] = term
            part16[tower, :, :, where] = term.astype(BF16)
            return carry

        lax.fori_loop(0, embed // tile, y_tile, 0)
        got_part[tower] = [
            send(part16.at[tower, (me_f + k) % groups], part_in.at[tower, k - 1],
                 me_dp, (me_f + k) % groups)
            for k in range(1, groups)
        ]

    def feat_pair(place):
        return feats.at[pl.ds(place * SIDE, SIDE)]

    beside = depth * SIDE + (1 - side)
    feats[me_dp] = cols[side]
    send(cols.at[1 - side], feats.at[me_dp], beside, me_f).wait_recv()
    line_step(0, feat_pair, 0)
    if depth_n > 2:
        line_step(0, feat_pair, 1)

    def y_rows(tower):
        for copy in got_part[tower]:
            copy.wait_recv()
        total = part[tower, me_f]
        for k in range(1, groups):
            total = total + part_in[tower, k - 1].astype(F32)
        y_keep[tower] = total
        norm_factor, _ = factor(total)
        return (total * norm_factor).astype(BF16)

    z_txt[depth] = y_rows(1)
    got_txt = [
        send(z_txt.at[depth], z_txt.at[depth], at_depth(k) * SIDE + side, me_f)
        for k in range(1, depth_n)
    ]
    z_img[spot] = y_rows(0)
    got_img = [
        send(z_img.at[spot], z_img.at[spot], *at_spot(k)) for k in range(1, plane_n)
    ]
    for step in range(2, depth_n - 1):
        line_step(0, feat_pair, step)
    for copy in got_txt + got_img:
        copy.wait_recv()

    n_img, n_txt = plane_n * rows, depth_n * rows
    scale = jnp.exp(jnp.full((1, n_txt), log_temp[0], F32))
    scores = dot(
        z_img[...].reshape(n_img, embed), z_txt[...].reshape(n_txt, embed), 1, 1
    )
    scores = scale * scores + bias[0]
    row = lax.broadcasted_iota(jnp.int32, (n_img, n_txt), 0) - spot * rows
    col = lax.broadcasted_iota(jnp.int32, (n_img, n_txt), 1) - depth * rows
    label = jnp.where((row == col) & (row >= 0) & (row < rows), 1.0, -1.0).astype(F32)
    pair = (scale * (-label * jax.nn.sigmoid(-label * scores))).astype(BF16)

    def txt_tile(j, carry):
        where = lanes(j, tile)
        term = dot(pair, z_img[:, :, where].reshape(n_img, tile), 0, 0)
        term = term.reshape(depth_n, rows, tile)
        d_txt[:, :, where] = term
        d_txt16[:, :, where] = term.astype(BF16)
        return carry

    lax.fori_loop(0, embed // tile, txt_tile, 0)
    got_txt = [
        send(d_txt16.at[at_depth(k)], d_txt_in.at[k - 1], at_depth(k) * SIDE + side, me_f)
        for k in range(1, depth_n)
    ]

    def img_tile(j, carry):
        where = lanes(j, tile)
        term = dot(pair, z_txt[:, :, where].reshape(n_txt, tile), 1, 0)
        term = term.reshape(plane_n, rows, tile)
        d_img[:, :, where] = term
        d_img16[:, :, where] = term.astype(BF16)
        return carry

    lax.fori_loop(0, embed // tile, img_tile, 0)
    got_img = [
        send(d_img16.at[(spot + k) % plane_n], d_img_in.at[k - 1], *at_spot(k))
        for k in range(1, plane_n)
    ]

    for tower, copies, own, arrived in (
        (1, got_txt, d_txt[depth], d_txt_in),
        (0, got_img, d_img[spot], d_img_in),
    ):
        for k, copy in enumerate(copies):
            copy.wait_recv()
            own = own + arrived[k].astype(F32)
        dy[tower] = back_norm(y_keep[tower], own)

    got_dy = []
    for k in range(1, dp_n):
        to_dp = (me_dp + k) % dp_n
        got_dy.append(
            send(dy.at[to_dp % SIDE, :, lanes(to_dp // SIDE, tall)], dy_all.at[me_f, me_dp],
                 to_dp, me_f)
        )
    dy_all[me_f, me_dp] = dy[side, :, lanes(depth, tall)]
    line_step(0, feat_pair, depth_n - 1)
    for copy in got_dy:
        copy.wait_recv()
    half = groups // 2
    across = (me_f + half) % groups
    twin = me_f + 1 - 2 * (me_f % 2)
    from_across = send(dy_all.at[me_f], dy_all.at[me_f], me_dp, across)
    from_twin = send(dy_all.at[me_f], dy_all.at[me_f], me_dp, twin)

    def grad_of(group):
        left = feats[:, group].reshape(dp_n * rows, wide)
        return dot(left, dy_all[group].reshape(dp_n * rows, tall), 0, 0)

    grad = grad_of(me_f)
    from_twin.wait_recv()
    grad = grad + grad_of(twin)
    from_across.wait_recv()
    passed_on = send(dy_all.at[across], dy_all.at[across], me_dp, twin)
    grad = grad + grad_of(across)
    passed_on.wait_recv()
    grad = grad + grad_of((twin + half) % groups)
    def out_tile(place):
        return out.at[side, :, lanes(place, tall)]

    def over_hop(way, step, place):
        return pltpu.make_async_remote_copy(
            src_ref=out_tile(place), dst_ref=out_tile(place),
            send_sem=over_send.at[(way + 1) // 2, step],
            recv_sem=over_recv.at[(way + 1) // 2, step],
            device_id=(beside, me_f), device_id_type=pl.DeviceIdType.MESH,
        )

    out[side, :, lanes(depth, tall)] = grad.astype(BF16)
    for step in range(depth_n):
        line_step(1, out_tile, step, lambda *at: over_hop(*at).start())
    for step in range(depth_n):
        for way in (-1, 1):
            if step > 0 or way > 0:
                @pl.when(on_line(depth + way * step))
                def _(way=way, step=step):
                    over_hop(way, step, depth + way * step).wait()
    line_sent(0, feat_pair)
    line_sent(1, out_tile)
    for copy in sent:
        copy.wait_send()


def in_one_kernel(dp_n, groups, img_feat, txt_feat, img_weight, txt_weight, log_temp, bias):
    rows, width = img_feat.shape
    wide, embed = img_weight.shape
    depth_n, plane_n = dp_n // SIDE, SIDE * groups
    tall = embed // depth_n
    copies = 2 * 2 * (groups - 1) + dp_n - 1 + 4 + 2 * (depth_n - 1 + plane_n - 1)
    hbm = pl.BlockSpec(memory_space=pltpu.HBM)
    vmem = pl.BlockSpec(memory_space=pltpu.VMEM)
    smem = pl.BlockSpec(memory_space=pltpu.SMEM)
    tiles = pl.pallas_call(
        functools.partial(kernel, (dp_n, groups, rows, width, embed)),
        out_shape=jax.ShapeDtypeStruct((SIDE, wide, embed), BF16),
        in_specs=[hbm] * 4 + [smem] * 2,
        out_specs=vmem,
        scratch_shapes=[
            pltpu.VMEM((wide, embed), BF16),
            pltpu.VMEM((wide, embed), BF16),
            pltpu.VMEM((2, groups, rows, wide), BF16),
            pltpu.VMEM((dp_n, groups, rows, wide), BF16),
            pltpu.VMEM((2, groups, rows, embed), F32),
            pltpu.VMEM((2, groups, rows, embed), BF16),
            pltpu.VMEM((2, groups - 1, rows, embed), BF16),
            pltpu.VMEM((2, rows, embed), F32),
            pltpu.VMEM((plane_n, rows, embed), BF16),
            pltpu.VMEM((depth_n, rows, embed), BF16),
            pltpu.VMEM((plane_n, rows, embed), F32),
            pltpu.VMEM((plane_n, rows, embed), BF16),
            pltpu.VMEM((plane_n - 1, rows, embed), BF16),
            pltpu.VMEM((depth_n, rows, embed), F32),
            pltpu.VMEM((depth_n, rows, embed), BF16),
            pltpu.VMEM((depth_n - 1, rows, embed), BF16),
            pltpu.VMEM((2, rows, embed), BF16),
            pltpu.VMEM((groups, dp_n, rows, tall), BF16),
            pltpu.SemaphoreType.DMA((copies,)),
            pltpu.SemaphoreType.DMA((copies,)),
            pltpu.SemaphoreType.DMA((4,)),
            pltpu.SemaphoreType.DMA((2, 2, depth_n)),
            pltpu.SemaphoreType.DMA((2, 2, depth_n)),
            pltpu.SemaphoreType.DMA((2, depth_n)),
            pltpu.SemaphoreType.DMA((2, depth_n)),
        ],
        compiler_params=pltpu.CompilerParams(
            collective_id=0, has_side_effects=True, vmem_limit_bytes=48 * 2**20
        ),
    )(img_feat, txt_feat, img_weight, txt_weight, log_temp, bias)
    return (tiles[0].astype(F32), tiles[1].astype(F32))


def on_device(dp_n, groups, img_feat, txt_feat, img_weight, txt_weight, log_temp, bias):
    arrays = (img_feat, txt_feat, img_weight, txt_weight, log_temp, bias)
    rows = img_feat.shape[0]
    wide, embed = img_weight.shape
    depth_n = dp_n // SIDE
    held = embed * rows * (12 * SIDE * groups + 10 * depth_n + 28 * groups)
    held += 2 * rows * dp_n * groups * (wide + embed // depth_n) + 12 * wide * embed
    if (
        dp_n % SIDE or groups != 4 or rows % 16 or wide % 128
        or embed % (128 * depth_n) or held > 40 * 2**20
    ):
        return by_collectives(*arrays)
    return in_one_kernel(dp_n, groups, *arrays)


def solution(mesh):
    placed = (
        P(("dp", "fsdp"), None),
        P(("dp", "fsdp"), None),
        P("fsdp", None),
        P("fsdp", None),
        P(),
        P(),
    )
    return jax.shard_map(
        functools.partial(on_device, mesh.shape["dp"], mesh.shape["fsdp"]),
        mesh=mesh,
        in_specs=placed,
        out_specs=(P("fsdp", None), P("fsdp", None)),
        check_vma=False,
    )
```

```python
import functools

import jax
import jax.numpy as jnp
from jax import lax
from jax.experimental import pallas as pl
from jax.experimental.pallas import tpu as pltpu
from jax.sharding import PartitionSpec as P

EPS = 1e-06


def factor(y_rows):
    mean_sq = jnp.mean(y_rows * y_rows, -1, keepdims=True)
    return (lax.rsqrt(mean_sq + EPS) * y_rows.shape[-1] ** (-0.5), mean_sq)


def back_norm(y_rows, grad_rows):
    norm_factor, mean_sq = factor(y_rows)
    inner_sum = jnp.sum(y_rows * grad_rows, -1, keepdims=True)
    result = norm_factor * grad_rows - norm_factor * y_rows * inner_sum / (
        y_rows.shape[-1] * (mean_sq + EPS)
    )
    return result.astype(jnp.bfloat16)


def by_collectives(img_feat, txt_feat, img_weight, txt_weight, log_temp, bias):
    row_count = img_feat.shape[0]
    groups = lax.axis_size("fsdp")
    dp_index = lax.axis_index("dp")
    fsdp_index = lax.axis_index("fsdp")
    img_cols, txt_cols = (
        lax.all_to_all(img_feat, "fsdp", split_axis=1, concat_axis=0, tiled=True),
        lax.all_to_all(txt_feat, "fsdp", split_axis=1, concat_axis=0, tiled=True),
    )
    y_img = jnp.dot(
        img_feat,
        lax.all_gather(img_weight, "fsdp", axis=0, tiled=True),
        preferred_element_type=jnp.float32,
    )
    y_txt = jnp.dot(
        txt_feat,
        lax.all_gather(txt_weight, "fsdp", axis=0, tiled=True),
        preferred_element_type=jnp.float32,
    )
    img_factor, unused_img = factor(y_img)
    z_own = (y_img * img_factor).astype(jnp.bfloat16)
    image_block = lax.all_gather(z_own, "fsdp", axis=0, tiled=True)
    txt_factor, unused_txt = factor(y_txt)
    z_txt = (y_txt * txt_factor).astype(jnp.bfloat16)
    temp_scale = jnp.exp(log_temp[0])
    bias_value = bias[0]
    group_rows = image_block.shape[0]
    image_ids = dp_index * groups * row_count + jnp.arange(group_rows, dtype=jnp.int32)
    text_piece = lax.all_gather(z_txt, "dp", axis=0, tiled=True)
    length = text_piece.shape[0]
    text_pos = jnp.arange(length, dtype=jnp.int32)
    text_ids = (text_pos // row_count * groups + fsdp_index) * row_count + text_pos % row_count
    logits = (
        temp_scale
        * lax.dot_general(
            image_block, text_piece, (((1,), (1,)), ((), ())), preferred_element_type=jnp.float32
        )
        + bias_value
    )
    pair_label = jnp.where(image_ids[:, None] == text_ids[None, :], 1.0, -1.0).astype(jnp.float32)
    pair_weight = (temp_scale * (-pair_label * jax.nn.sigmoid(-pair_label * logits))).astype(
        jnp.bfloat16
    )
    grad_sum = jnp.dot(pair_weight, text_piece, preferred_element_type=jnp.float32)
    grad_txt = lax.psum_scatter(
        lax.dot_general(
            pair_weight, image_block, (((0,), (0,)), ((), ())), preferred_element_type=jnp.float32
        ),
        "dp",
        scatter_dimension=0,
        tiled=True,
    )
    grad_img = lax.psum_scatter(grad_sum, "fsdp", scatter_dimension=0, tiled=True)
    dy_img = back_norm(y_img, grad_img)
    dy_txt = back_norm(y_txt, grad_txt)
    dy_img_group, dy_txt_group = (
        lax.all_gather(dy_img, "fsdp", axis=0, tiled=True),
        lax.all_gather(dy_txt, "fsdp", axis=0, tiled=True),
    )
    weight_img = lax.dot_general(
        img_cols, dy_img_group, (((0,), (0,)), ((), ())), preferred_element_type=jnp.float32
    )
    weight_txt = lax.dot_general(
        txt_cols, dy_txt_group, (((0,), (0,)), ((), ())), preferred_element_type=jnp.float32
    )
    grad_img_weight, grad_txt_weight = lax.psum((weight_img, weight_txt), "dp")
    return (grad_img_weight, grad_txt_weight)


BF16 = jnp.bfloat16
F32 = jnp.float32
SIDE = 2
CHUNKS = 3


def dot(a, b, a_dim, b_dim):
    return lax.dot_general(a, b, (((a_dim,), (b_dim,)), ((), ())), preferred_element_type=F32)


def kernel(
    dims, img, txt, w_img_hbm, w_txt_hbm, log_temp, bias, out,
    w_img, w_txt, cols, feats, part, pre_in, pre16, twin_in, part_in, y_keep, z_img, z_txt,
    d_img, d_img16, d_img_in, d_txt, d_txt16, d_txt_in, dy, dy_all,
    send_sem, recv_sem, local_sem, line_send, line_recv, over_send, over_recv,
):
    dp_n, groups, rows, width, embed = dims
    depth_n = dp_n // SIDE
    plane_n = SIDE * groups
    wide, tall = width // groups, embed // depth_n
    me_dp, me_f = lax.axis_index("dp"), lax.axis_index("fsdp")
    depth, side = me_dp // SIDE, me_dp % SIDE
    spot = side * groups + me_f
    count = [0]

    def send(source, target, to_dp, to_f):
        number = count[0]
        count[0] += 1
        copy = pltpu.make_async_remote_copy(
            src_ref=source, dst_ref=target,
            send_sem=send_sem.at[number], recv_sem=recv_sem.at[number],
            device_id=(to_dp, to_f), device_id_type=pl.DeviceIdType.MESH,
        )
        copy.start()
        sent.append(copy)
        return copy

    sent = []

    def at_spot(k):
        other = (spot + k) % plane_n
        return depth * SIDE + other // groups, other % groups

    def at_depth(k):
        return (depth + k) % depth_n

    def lanes(start, size):
        return pl.ds(pl.multiple_of(start * size, size), size)

    def line_hop(use, view, way, step):
        place, to = depth + way * step, depth - way
        return pltpu.make_async_remote_copy(
            src_ref=view(place), dst_ref=view(place),
            send_sem=line_send.at[use, (way + 1) // 2, step],
            recv_sem=line_recv.at[use, (way + 1) // 2, step],
            device_id=(to * SIDE + side, me_f), device_id_type=pl.DeviceIdType.MESH,
        )

    def on_line(place):
        return (place >= 0) & (place < depth_n)

    def line_step(use, view, step, then=None):
        for way in (-1, 1):
            place, to = depth + way * step, depth - way

            if step > 0:
                @pl.when(on_line(place))
                def _(way=way):
                    line_hop(use, view, way, step - 1).wait_recv()

            if step < depth_n - 1:
                @pl.when(on_line(place) & on_line(to))
                def _(way=way):
                    line_hop(use, view, way, step).start()

            if then is not None and (step > 0 or way > 0):
                @pl.when(on_line(place))
                def _(way=way, place=place):
                    then(way, step, place)

    def line_sent(use, view):
        for step in range(depth_n - 1):
            for way in (-1, 1):
                @pl.when(on_line(depth + way * step) & on_line(depth - way))
                def _(way=way, step=step):
                    line_hop(use, view, way, step).wait_send()

    own_copies = [
        pltpu.make_async_copy(img.at[:, lanes(me_f, wide)], cols.at[0, me_f], local_sem.at[0]),
        pltpu.make_async_copy(txt.at[:, lanes(me_f, wide)], cols.at[1, me_f], local_sem.at[1]),
        pltpu.make_async_copy(w_img_hbm, w_img, local_sem.at[2]),
        pltpu.make_async_copy(w_txt_hbm, w_txt, local_sem.at[3]),
    ]
    for copy in own_copies:
        copy.start()

    barrier = pltpu.get_barrier_semaphore()
    peers = [at_spot(k) for k in range(1, plane_n)]
    peers += [
        (at_depth(k) * SIDE + s, me_f) for k in range(1, depth_n) for s in range(SIDE)
    ]
    for peer in peers:
        pl.semaphore_signal(barrier, inc=1, device_id=peer, device_id_type=pl.DeviceIdType.MESH)
    pl.semaphore_wait(barrier, len(peers))

    got_cols = []
    for tower, feat in ((1, txt), (0, img)):
        for k in range(1, groups):
            to_f = (me_f + k) % groups
            got_cols.append(
                send(feat.at[:, lanes(to_f, wide)], cols.at[tower, me_f], me_dp, to_f)
            )
    for copy in own_copies:
        copy.wait()

    for copy in got_cols:
        copy.wait_recv()

    def feat_pair(place):
        return feats.at[pl.ds(place * SIDE, SIDE)]

    beside = depth * SIDE + (1 - side)
    feat_beside = send(cols.at[1 - side], feats.at[me_dp], beside, me_f)

    half = groups // 2
    core = me_f % half
    across = (me_f + half) % groups
    twin = me_f + 1 - 2 * core
    away = across - core
    tile = 384 if embed % 384 == 0 else 128
    got_pre, got_twin, got_part = {}, {}, {}
    for tower, weight in ((1, w_txt), (0, w_img)):

        def y_tile(j, carry, tower=tower, weight=weight):
            where = lanes(j, tile)
            term = dot(cols[tower].reshape(groups * rows, wide), weight[:, where], 1, 0)
            part[tower, :, :, where] = term.reshape(groups, rows, tile)
            return carry

        lax.fori_loop(0, embed // tile, y_tile, 0)
        got_pre[tower] = send(
            part.at[tower, pl.ds(away, half), :, lanes(1 - core, embed // half)],
            pre_in.at[tower], me_dp, twin,
        )
        got_twin[tower] = send(part.at[tower, twin], twin_in.at[tower], me_dp, twin)
    for tower in (1, 0):
        got_pre[tower].wait_recv()
        mine = part[tower, pl.ds(away, half), :, lanes(core, embed // half)]
        pre16[tower] = (mine + pre_in[tower]).astype(BF16)
        got_part[tower] = [
            send(pre16.at[tower, n], part_in.at[tower, :, lanes(core, embed // half)],
                 me_dp, away + n)
            for n in ((core + k) % half for k in range(half))
        ]
    feats[me_dp] = cols[side]
    feat_beside.wait_recv()
    line_step(0, feat_pair, 0)

    def y_rows(tower):
        got_twin[tower].wait_recv()
        for copy in got_part[tower]:
            copy.wait_recv()
        total = part[tower, me_f] + twin_in[tower] + part_in[tower].astype(F32)
        y_keep[tower] = total
        norm_factor, _ = factor(total)
        return (total * norm_factor).astype(BF16)

    z_txt[depth] = y_rows(1)
    got_txt = [
        send(z_txt.at[depth], z_txt.at[depth], at_depth(k) * SIDE + side, me_f)
        for k in range(1, depth_n)
    ]
    z_img[spot] = y_rows(0)
    got_img = [
        send(z_img.at[spot], z_img.at[spot], *at_spot(k)) for k in range(1, plane_n)
    ]
    if depth_n > 2:
        line_step(0, feat_pair, 1)
    for copy in got_txt + got_img:
        copy.wait_recv()
    for step in range(2, depth_n - 1):
        line_step(0, feat_pair, step)

    n_img, n_txt = plane_n * rows, depth_n * rows
    scale = jnp.exp(jnp.full((1, n_txt), log_temp[0], F32))
    scores = dot(
        z_img[...].reshape(n_img, embed), z_txt[...].reshape(n_txt, embed), 1, 1
    )
    scores = scale * scores + bias[0]
    row = lax.broadcasted_iota(jnp.int32, (n_img, n_txt), 0) - spot * rows
    col = lax.broadcasted_iota(jnp.int32, (n_img, n_txt), 1) - depth * rows
    label = jnp.where((row == col) & (row >= 0) & (row < rows), 1.0, -1.0).astype(F32)
    pair = (scale * (-label * jax.nn.sigmoid(-label * scores))).astype(BF16)

    def txt_tile(j, carry):
        where = lanes(j, tile)
        term = dot(pair, z_img[:, :, where].reshape(n_img, tile), 0, 0)
        term = term.reshape(depth_n, rows, tile)
        d_txt[:, :, where] = term
        d_txt16[:, :, where] = term.astype(BF16)
        return carry

    lax.fori_loop(0, embed // tile, txt_tile, 0)
    got_txt = [
        send(d_txt16.at[at_depth(k)], d_txt_in.at[k - 1], at_depth(k) * SIDE + side, me_f)
        for k in range(1, depth_n)
    ]

    def img_tile(j, carry):
        where = lanes(j, tile)
        term = dot(pair, z_txt[:, :, where].reshape(n_txt, tile), 1, 0)
        term = term.reshape(plane_n, rows, tile)
        d_img[:, :, where] = term
        d_img16[:, :, where] = term.astype(BF16)
        return carry

    lax.fori_loop(0, embed // tile, img_tile, 0)
    got_img = [
        send(d_img16.at[(spot + k) % plane_n], d_img_in.at[k - 1], *at_spot(k))
        for k in range(1, plane_n)
    ]

    for tower, copies, own, arrived in (
        (1, got_txt, d_txt[depth], d_txt_in),
        (0, got_img, d_img[spot], d_img_in),
    ):
        for k, copy in enumerate(copies):
            copy.wait_recv()
            own = own + arrived[k].astype(F32)
        dy[tower] = back_norm(y_keep[tower], own)

    got_dy = []
    for k in range(1, dp_n):
        to_dp = (me_dp + k) % dp_n
        got_dy.append(
            send(dy.at[to_dp % SIDE, :, lanes(to_dp // SIDE, tall)], dy_all.at[me_f, me_dp],
                 to_dp, me_f)
        )
    dy_all[me_f, me_dp] = dy[side, :, lanes(depth, tall)]
    line_step(0, feat_pair, depth_n - 1)
    for copy in got_dy:
        copy.wait_recv()
    from_across = send(dy_all.at[me_f], dy_all.at[me_f], me_dp, across)
    from_twin = send(dy_all.at[me_f], dy_all.at[me_f], me_dp, twin)

    def grad_of(group):
        left = feats[:, group].reshape(dp_n * rows, wide)
        return dot(left, dy_all[group].reshape(dp_n * rows, tall), 0, 0)

    grad = grad_of(me_f)
    from_twin.wait_recv()
    grad = grad + grad_of(twin)
    from_across.wait_recv()
    passed_on = send(dy_all.at[across], dy_all.at[across], me_dp, twin)
    grad = grad + grad_of(across)
    passed_on.wait_recv()
    grad = grad + grad_of((twin + half) % groups)
    def out_tile(chunk):
        deep = wide // CHUNKS
        return lambda place: out.at[side, pl.ds(chunk * deep, deep), lanes(place, tall)]

    def over_hop(chunk, way, step, place):
        return pltpu.make_async_remote_copy(
            src_ref=out_tile(chunk)(place), dst_ref=out_tile(chunk)(place),
            send_sem=over_send.at[chunk, (way + 1) // 2, step],
            recv_sem=over_recv.at[chunk, (way + 1) // 2, step],
            device_id=(beside, me_f), device_id_type=pl.DeviceIdType.MESH,
        )

    out[side, :, lanes(depth, tall)] = grad.astype(BF16)
    for step in range(depth_n):
        for chunk in range(CHUNKS):
            line_step(1 + chunk, out_tile(chunk), step,
                      lambda *at, chunk=chunk: over_hop(chunk, *at).start())
    for step in range(depth_n):
        for way in (-1, 1):
            if step > 0 or way > 0:
                @pl.when(on_line(depth + way * step))
                def _(way=way, step=step):
                    for chunk in range(CHUNKS):
                        over_hop(chunk, way, step, depth + way * step).wait()
    line_sent(0, feat_pair)
    for chunk in range(CHUNKS):
        line_sent(1 + chunk, out_tile(chunk))
    for copy in sent:
        copy.wait_send()


def in_one_kernel(dp_n, groups, img_feat, txt_feat, img_weight, txt_weight, log_temp, bias):
    rows, width = img_feat.shape
    wide, embed = img_weight.shape
    depth_n, plane_n = dp_n // SIDE, SIDE * groups
    tall = embed // depth_n
    copies = 2 * (groups - 1) + 8 + dp_n - 1 + 4 + 2 * (depth_n - 1 + plane_n - 1)
    hbm = pl.BlockSpec(memory_space=pltpu.HBM)
    vmem = pl.BlockSpec(memory_space=pltpu.VMEM)
    smem = pl.BlockSpec(memory_space=pltpu.SMEM)
    tiles = pl.pallas_call(
        functools.partial(kernel, (dp_n, groups, rows, width, embed)),
        out_shape=jax.ShapeDtypeStruct((SIDE, wide, embed), BF16),
        in_specs=[hbm] * 4 + [smem] * 2,
        out_specs=vmem,
        scratch_shapes=[
            pltpu.VMEM((wide, embed), BF16),
            pltpu.VMEM((wide, embed), BF16),
            pltpu.VMEM((2, groups, rows, wide), BF16),
            pltpu.VMEM((dp_n, groups, rows, wide), BF16),
            pltpu.VMEM((2, groups, rows, embed), F32),
            pltpu.VMEM((2, groups // 2, rows, embed // 2), F32),
            pltpu.VMEM((2, groups // 2, rows, embed // 2), BF16),
            pltpu.VMEM((2, rows, embed), F32),
            pltpu.VMEM((2, rows, embed), BF16),
            pltpu.VMEM((2, rows, embed), F32),
            pltpu.VMEM((plane_n, rows, embed), BF16),
            pltpu.VMEM((depth_n, rows, embed), BF16),
            pltpu.VMEM((plane_n, rows, embed), F32),
            pltpu.VMEM((plane_n, rows, embed), BF16),
            pltpu.VMEM((plane_n - 1, rows, embed), BF16),
            pltpu.VMEM((depth_n, rows, embed), F32),
            pltpu.VMEM((depth_n, rows, embed), BF16),
            pltpu.VMEM((depth_n - 1, rows, embed), BF16),
            pltpu.VMEM((2, rows, embed), BF16),
            pltpu.VMEM((groups, dp_n, rows, tall), BF16),
            pltpu.SemaphoreType.DMA((copies,)),
            pltpu.SemaphoreType.DMA((copies,)),
            pltpu.SemaphoreType.DMA((4,)),
            pltpu.SemaphoreType.DMA((1 + CHUNKS, 2, depth_n)),
            pltpu.SemaphoreType.DMA((1 + CHUNKS, 2, depth_n)),
            pltpu.SemaphoreType.DMA((CHUNKS, 2, depth_n)),
            pltpu.SemaphoreType.DMA((CHUNKS, 2, depth_n)),
        ],
        compiler_params=pltpu.CompilerParams(
            collective_id=0, has_side_effects=True, vmem_limit_bytes=61 * 2**20
        ),
    )(img_feat, txt_feat, img_weight, txt_weight, log_temp, bias)
    return (tiles[0].astype(F32), tiles[1].astype(F32))


def on_device(dp_n, groups, img_feat, txt_feat, img_weight, txt_weight, log_temp, bias):
    arrays = (img_feat, txt_feat, img_weight, txt_weight, log_temp, bias)
    rows = img_feat.shape[0]
    wide, embed = img_weight.shape
    depth_n = dp_n // SIDE
    held = embed * rows * (12 * SIDE * groups + 10 * depth_n + 28 * groups)
    held += 2 * rows * dp_n * groups * (wide + embed // depth_n) + 12 * wide * embed
    if (
        dp_n % SIDE or groups != 4 or rows % 16 or wide % 128 or wide % (16 * CHUNKS)
        or embed % 256
        or embed % (128 * depth_n) or held > 40 * 2**20
    ):
        return by_collectives(*arrays)
    return in_one_kernel(dp_n, groups, *arrays)


def solution(mesh):
    placed = (
        P(("dp", "fsdp"), None),
        P(("dp", "fsdp"), None),
        P("fsdp", None),
        P("fsdp", None),
        P(),
        P(),
    )
    return jax.shard_map(
        functools.partial(on_device, mesh.shape["dp"], mesh.shape["fsdp"]),
        mesh=mesh,
        in_specs=placed,
        out_specs=(P("fsdp", None), P("fsdp", None)),
        check_vma=False,
    )
```

```python
import functools

import jax
import jax.numpy as jnp
from jax import lax
from jax.experimental import pallas as pl
from jax.experimental.pallas import tpu as pltpu
from jax.sharding import PartitionSpec as P

EPS = 1e-06


def factor(y_rows):
    mean_sq = jnp.mean(y_rows * y_rows, -1, keepdims=True)
    return (lax.rsqrt(mean_sq + EPS) * y_rows.shape[-1] ** (-0.5), mean_sq)


def back_norm(y_rows, grad_rows):
    norm_factor, mean_sq = factor(y_rows)
    inner_sum = jnp.sum(y_rows * grad_rows, -1, keepdims=True)
    result = norm_factor * grad_rows - norm_factor * y_rows * inner_sum / (
        y_rows.shape[-1] * (mean_sq + EPS)
    )
    return result.astype(jnp.bfloat16)


def by_collectives(img_feat, txt_feat, img_weight, txt_weight, log_temp, bias):
    row_count = img_feat.shape[0]
    groups = lax.axis_size("fsdp")
    dp_index = lax.axis_index("dp")
    fsdp_index = lax.axis_index("fsdp")
    img_cols, txt_cols = (
        lax.all_to_all(img_feat, "fsdp", split_axis=1, concat_axis=0, tiled=True),
        lax.all_to_all(txt_feat, "fsdp", split_axis=1, concat_axis=0, tiled=True),
    )
    y_img = jnp.dot(
        img_feat,
        lax.all_gather(img_weight, "fsdp", axis=0, tiled=True),
        preferred_element_type=jnp.float32,
    )
    y_txt = jnp.dot(
        txt_feat,
        lax.all_gather(txt_weight, "fsdp", axis=0, tiled=True),
        preferred_element_type=jnp.float32,
    )
    img_factor, unused_img = factor(y_img)
    z_own = (y_img * img_factor).astype(jnp.bfloat16)
    image_block = lax.all_gather(z_own, "fsdp", axis=0, tiled=True)
    txt_factor, unused_txt = factor(y_txt)
    z_txt = (y_txt * txt_factor).astype(jnp.bfloat16)
    temp_scale = jnp.exp(log_temp[0])
    bias_value = bias[0]
    group_rows = image_block.shape[0]
    image_ids = dp_index * groups * row_count + jnp.arange(group_rows, dtype=jnp.int32)
    text_piece = lax.all_gather(z_txt, "dp", axis=0, tiled=True)
    length = text_piece.shape[0]
    text_pos = jnp.arange(length, dtype=jnp.int32)
    text_ids = (text_pos // row_count * groups + fsdp_index) * row_count + text_pos % row_count
    logits = (
        temp_scale
        * lax.dot_general(
            image_block, text_piece, (((1,), (1,)), ((), ())), preferred_element_type=jnp.float32
        )
        + bias_value
    )
    pair_label = jnp.where(image_ids[:, None] == text_ids[None, :], 1.0, -1.0).astype(jnp.float32)
    pair_weight = (temp_scale * (-pair_label * jax.nn.sigmoid(-pair_label * logits))).astype(
        jnp.bfloat16
    )
    grad_sum = jnp.dot(pair_weight, text_piece, preferred_element_type=jnp.float32)
    grad_txt = lax.psum_scatter(
        lax.dot_general(
            pair_weight, image_block, (((0,), (0,)), ((), ())), preferred_element_type=jnp.float32
        ),
        "dp",
        scatter_dimension=0,
        tiled=True,
    )
    grad_img = lax.psum_scatter(grad_sum, "fsdp", scatter_dimension=0, tiled=True)
    dy_img = back_norm(y_img, grad_img)
    dy_txt = back_norm(y_txt, grad_txt)
    dy_img_group, dy_txt_group = (
        lax.all_gather(dy_img, "fsdp", axis=0, tiled=True),
        lax.all_gather(dy_txt, "fsdp", axis=0, tiled=True),
    )
    weight_img = lax.dot_general(
        img_cols, dy_img_group, (((0,), (0,)), ((), ())), preferred_element_type=jnp.float32
    )
    weight_txt = lax.dot_general(
        txt_cols, dy_txt_group, (((0,), (0,)), ((), ())), preferred_element_type=jnp.float32
    )
    grad_img_weight, grad_txt_weight = lax.psum((weight_img, weight_txt), "dp")
    return (grad_img_weight, grad_txt_weight)


BF16 = jnp.bfloat16
F32 = jnp.float32
SIDE = 2
CHUNKS = 3


def dot(a, b, a_dim, b_dim):
    return lax.dot_general(a, b, (((a_dim,), (b_dim,)), ((), ())), preferred_element_type=F32)


def kernel(
    dims, img, txt, w_img_hbm, w_txt_hbm, log_temp, bias, out,
    w_img, w_txt, cols, feats, part, pre_in, pre16, twin_in, part_in, y_keep, z_img, z_txt,
    d_img, d_img16, d_img_in, d_txt, d_txt16, d_txt_in, dy, dy_all,
    send_sem, recv_sem, local_sem, line_send, line_recv, over_send, over_recv,
):
    dp_n, groups, rows, width, embed = dims
    depth_n = dp_n // SIDE
    plane_n = SIDE * groups
    wide, tall = width // groups, embed // depth_n
    me_dp, me_f = lax.axis_index("dp"), lax.axis_index("fsdp")
    depth, side = me_dp // SIDE, me_dp % SIDE
    spot = side * groups + me_f
    count = [0]

    def send(source, target, to_dp, to_f):
        number = count[0]
        count[0] += 1
        copy = pltpu.make_async_remote_copy(
            src_ref=source, dst_ref=target,
            send_sem=send_sem.at[number], recv_sem=recv_sem.at[number],
            device_id=(to_dp, to_f), device_id_type=pl.DeviceIdType.MESH,
        )
        copy.start()
        sent.append(copy)
        return copy

    sent = []

    def at_spot(k):
        other = (spot + k) % plane_n
        return depth * SIDE + other // groups, other % groups

    def at_depth(k):
        return (depth + k) % depth_n

    def lanes(start, size):
        return pl.ds(pl.multiple_of(start * size, size), size)

    def line_hop(use, view, way, step):
        place, to = depth + way * step, depth - way
        return pltpu.make_async_remote_copy(
            src_ref=view(place), dst_ref=view(place),
            send_sem=line_send.at[use, (way + 1) // 2, step],
            recv_sem=line_recv.at[use, (way + 1) // 2, step],
            device_id=(to * SIDE + side, me_f), device_id_type=pl.DeviceIdType.MESH,
        )

    def on_line(place):
        return (place >= 0) & (place < depth_n)

    def line_step(use, view, step, then=None):
        for way in (-1, 1):
            place, to = depth + way * step, depth - way

            if step > 0:
                @pl.when(on_line(place))
                def _(way=way):
                    line_hop(use, view, way, step - 1).wait_recv()

            if step < depth_n - 1:
                @pl.when(on_line(place) & on_line(to))
                def _(way=way):
                    line_hop(use, view, way, step).start()

            if then is not None and (step > 0 or way > 0):
                @pl.when(on_line(place))
                def _(way=way, place=place):
                    then(way, step, place)

    def line_sent(use, view):
        for step in range(depth_n - 1):
            for way in (-1, 1):
                @pl.when(on_line(depth + way * step) & on_line(depth - way))
                def _(way=way, step=step):
                    line_hop(use, view, way, step).wait_send()

    own_copies = [
        pltpu.make_async_copy(img.at[:, lanes(me_f, wide)], cols.at[0, me_f], local_sem.at[0]),
        pltpu.make_async_copy(txt.at[:, lanes(me_f, wide)], cols.at[1, me_f], local_sem.at[1]),
        pltpu.make_async_copy(w_img_hbm, w_img, local_sem.at[2]),
        pltpu.make_async_copy(w_txt_hbm, w_txt, local_sem.at[3]),
    ]
    for copy in own_copies:
        copy.start()

    barrier = pltpu.get_barrier_semaphore()
    peers = [at_spot(k) for k in range(1, plane_n)]
    peers += [
        (at_depth(k) * SIDE + s, me_f) for k in range(1, depth_n) for s in range(SIDE)
    ]
    for peer in peers:
        pl.semaphore_signal(barrier, inc=1, device_id=peer, device_id_type=pl.DeviceIdType.MESH)
    pl.semaphore_wait(barrier, len(peers))

    got_cols = []
    for tower, feat in ((1, txt), (0, img)):
        for k in range(1, groups):
            to_f = (me_f + k) % groups
            got_cols.append(
                send(feat.at[:, lanes(to_f, wide)], cols.at[tower, me_f], me_dp, to_f)
            )
    for copy in own_copies:
        copy.wait()

    for copy in got_cols:
        copy.wait_recv()

    def feat_own(place):
        return feats.at[place * SIDE + side]

    def feat_other(place):
        return feats.at[place * SIDE + 1 - side]

    beside = depth * SIDE + (1 - side)
    feat_beside = send(cols.at[1 - side], feats.at[me_dp], beside, me_f)
    feats[me_dp] = cols[side]
    line_step(0, feat_own, 0)

    half = groups // 2
    core = me_f % half
    across = (me_f + half) % groups
    twin = me_f + 1 - 2 * core
    away = across - core
    tile = 384 if embed % 384 == 0 else 128
    got_pre, got_twin, got_part = {}, {}, {}
    for tower, weight in ((1, w_txt), (0, w_img)):

        def y_tile(j, carry, tower=tower, weight=weight):
            where = lanes(j, tile)
            term = dot(cols[tower].reshape(groups * rows, wide), weight[:, where], 1, 0)
            part[tower, :, :, where] = term.reshape(groups, rows, tile)
            return carry

        lax.fori_loop(0, embed // tile, y_tile, 0)
        got_pre[tower] = send(
            part.at[tower, pl.ds(away, half), :, lanes(1 - core, embed // half)],
            pre_in.at[tower], me_dp, twin,
        )
        got_twin[tower] = send(part.at[tower, twin], twin_in.at[tower], me_dp, twin)
    feat_beside.wait_recv()
    line_step(1, feat_other, 0)
    for tower in (1, 0):
        got_pre[tower].wait_recv()
        mine = part[tower, pl.ds(away, half), :, lanes(core, embed // half)]
        pre16[tower] = (mine + pre_in[tower]).astype(BF16)
        got_part[tower] = [
            send(pre16.at[tower, n], part_in.at[tower, :, lanes(core, embed // half)],
                 me_dp, away + n)
            for n in ((core + k) % half for k in range(half))
        ]
    if depth_n > 2:
        line_step(0, feat_own, 1)
    def y_rows(tower):
        got_twin[tower].wait_recv()
        for copy in got_part[tower]:
            copy.wait_recv()
        total = part[tower, me_f] + twin_in[tower] + part_in[tower].astype(F32)
        y_keep[tower] = total
        norm_factor, _ = factor(total)
        return (total * norm_factor).astype(BF16)

    z_txt[depth] = y_rows(1)
    got_txt = [
        send(z_txt.at[depth], z_txt.at[depth], at_depth(k) * SIDE + side, me_f)
        for k in range(1, depth_n)
    ]
    z_img[spot] = y_rows(0)
    got_img = [
        send(z_img.at[spot], z_img.at[spot], *at_spot(k)) for k in range(1, plane_n)
    ]
    if depth_n > 2:
        line_step(1, feat_other, 1)
    for copy in got_txt + got_img:
        copy.wait_recv()
    for step in range(2, depth_n - 1):
        line_step(0, feat_own, step)
        line_step(1, feat_other, step)

    n_img, n_txt = plane_n * rows, depth_n * rows
    scale = jnp.exp(jnp.full((1, n_txt), log_temp[0], F32))
    scores = dot(
        z_img[...].reshape(n_img, embed), z_txt[...].reshape(n_txt, embed), 1, 1
    )
    scores = scale * scores + bias[0]
    row = lax.broadcasted_iota(jnp.int32, (n_img, n_txt), 0) - spot * rows
    col = lax.broadcasted_iota(jnp.int32, (n_img, n_txt), 1) - depth * rows
    label = jnp.where((row == col) & (row >= 0) & (row < rows), 1.0, -1.0).astype(F32)
    pair = (scale * (-label * jax.nn.sigmoid(-label * scores))).astype(BF16)

    def txt_tile(j, carry):
        where = lanes(j, tile)
        term = dot(pair, z_img[:, :, where].reshape(n_img, tile), 0, 0)
        term = term.reshape(depth_n, rows, tile)
        d_txt[:, :, where] = term
        d_txt16[:, :, where] = term.astype(BF16)
        return carry

    lax.fori_loop(0, embed // tile, txt_tile, 0)
    got_txt = [
        send(d_txt16.at[at_depth(k)], d_txt_in.at[k - 1], at_depth(k) * SIDE + side, me_f)
        for k in range(1, depth_n)
    ]

    def img_tile(j, carry):
        where = lanes(j, tile)
        term = dot(pair, z_txt[:, :, where].reshape(n_txt, tile), 1, 0)
        term = term.reshape(plane_n, rows, tile)
        d_img[:, :, where] = term
        d_img16[:, :, where] = term.astype(BF16)
        return carry

    lax.fori_loop(0, embed // tile, img_tile, 0)
    got_img = [
        send(d_img16.at[(spot + k) % plane_n], d_img_in.at[k - 1], *at_spot(k))
        for k in range(1, plane_n)
    ]

    for tower, copies, own, arrived in (
        (1, got_txt, d_txt[depth], d_txt_in),
        (0, got_img, d_img[spot], d_img_in),
    ):
        for k, copy in enumerate(copies):
            copy.wait_recv()
            own = own + arrived[k].astype(F32)
        dy[tower] = back_norm(y_keep[tower], own)

    got_dy = []
    for k in range(1, dp_n):
        to_dp = (me_dp + k) % dp_n
        got_dy.append(
            send(dy.at[to_dp % SIDE, :, lanes(to_dp // SIDE, tall)], dy_all.at[me_f, me_dp],
                 to_dp, me_f)
        )
    dy_all[me_f, me_dp] = dy[side, :, lanes(depth, tall)]
    line_step(0, feat_own, depth_n - 1)
    line_step(1, feat_other, depth_n - 1)
    for copy in got_dy:
        copy.wait_recv()
    from_across = send(dy_all.at[me_f], dy_all.at[me_f], me_dp, across)
    from_twin = send(dy_all.at[me_f], dy_all.at[me_f], me_dp, twin)

    def grad_of(group):
        left = feats[:, group].reshape(dp_n * rows, wide)
        return dot(left, dy_all[group].reshape(dp_n * rows, tall), 0, 0)

    grad = grad_of(me_f)
    from_twin.wait_recv()
    grad = grad + grad_of(twin)
    from_across.wait_recv()
    passed_on = send(dy_all.at[across], dy_all.at[across], me_dp, twin)
    grad = grad + grad_of(across)
    passed_on.wait_recv()
    grad = grad + grad_of((twin + half) % groups)
    def out_tile(chunk):
        deep = wide // CHUNKS
        return lambda place: out.at[side, pl.ds(chunk * deep, deep), lanes(place, tall)]

    def over_hop(chunk, way, step, place):
        return pltpu.make_async_remote_copy(
            src_ref=out_tile(chunk)(place), dst_ref=out_tile(chunk)(place),
            send_sem=over_send.at[chunk, (way + 1) // 2, step],
            recv_sem=over_recv.at[chunk, (way + 1) // 2, step],
            device_id=(beside, me_f), device_id_type=pl.DeviceIdType.MESH,
        )

    out[side, :, lanes(depth, tall)] = grad.astype(BF16)
    for step in range(depth_n):
        for chunk in range(CHUNKS):
            line_step(2 + chunk, out_tile(chunk), step,
                      lambda *at, chunk=chunk: over_hop(chunk, *at).start())
    for step in range(depth_n):
        for way in (-1, 1):
            if step > 0 or way > 0:
                @pl.when(on_line(depth + way * step))
                def _(way=way, step=step):
                    for chunk in range(CHUNKS):
                        over_hop(chunk, way, step, depth + way * step).wait()
    line_sent(0, feat_own)
    line_sent(1, feat_other)
    for chunk in range(CHUNKS):
        line_sent(2 + chunk, out_tile(chunk))
    for copy in sent:
        copy.wait_send()


def in_one_kernel(dp_n, groups, img_feat, txt_feat, img_weight, txt_weight, log_temp, bias):
    rows, width = img_feat.shape
    wide, embed = img_weight.shape
    depth_n, plane_n = dp_n // SIDE, SIDE * groups
    tall = embed // depth_n
    copies = 2 * (groups - 1) + 8 + dp_n - 1 + 4 + 2 * (depth_n - 1 + plane_n - 1)
    hbm = pl.BlockSpec(memory_space=pltpu.HBM)
    vmem = pl.BlockSpec(memory_space=pltpu.VMEM)
    smem = pl.BlockSpec(memory_space=pltpu.SMEM)
    tiles = pl.pallas_call(
        functools.partial(kernel, (dp_n, groups, rows, width, embed)),
        out_shape=jax.ShapeDtypeStruct((SIDE, wide, embed), BF16),
        in_specs=[hbm] * 4 + [smem] * 2,
        out_specs=vmem,
        scratch_shapes=[
            pltpu.VMEM((wide, embed), BF16),
            pltpu.VMEM((wide, embed), BF16),
            pltpu.VMEM((2, groups, rows, wide), BF16),
            pltpu.VMEM((dp_n, groups, rows, wide), BF16),
            pltpu.VMEM((2, groups, rows, embed), F32),
            pltpu.VMEM((2, groups // 2, rows, embed // 2), F32),
            pltpu.VMEM((2, groups // 2, rows, embed // 2), BF16),
            pltpu.VMEM((2, rows, embed), F32),
            pltpu.VMEM((2, rows, embed), BF16),
            pltpu.VMEM((2, rows, embed), F32),
            pltpu.VMEM((plane_n, rows, embed), BF16),
            pltpu.VMEM((depth_n, rows, embed), BF16),
            pltpu.VMEM((plane_n, rows, embed), F32),
            pltpu.VMEM((plane_n, rows, embed), BF16),
            pltpu.VMEM((plane_n - 1, rows, embed), BF16),
            pltpu.VMEM((depth_n, rows, embed), F32),
            pltpu.VMEM((depth_n, rows, embed), BF16),
            pltpu.VMEM((depth_n - 1, rows, embed), BF16),
            pltpu.VMEM((2, rows, embed), BF16),
            pltpu.VMEM((groups, dp_n, rows, tall), BF16),
            pltpu.SemaphoreType.DMA((copies,)),
            pltpu.SemaphoreType.DMA((copies,)),
            pltpu.SemaphoreType.DMA((4,)),
            pltpu.SemaphoreType.DMA((2 + CHUNKS, 2, depth_n)),
            pltpu.SemaphoreType.DMA((2 + CHUNKS, 2, depth_n)),
            pltpu.SemaphoreType.DMA((CHUNKS, 2, depth_n)),
            pltpu.SemaphoreType.DMA((CHUNKS, 2, depth_n)),
        ],
        compiler_params=pltpu.CompilerParams(
            collective_id=0, has_side_effects=True, vmem_limit_bytes=61 * 2**20
        ),
    )(img_feat, txt_feat, img_weight, txt_weight, log_temp, bias)
    return (tiles[0].astype(F32), tiles[1].astype(F32))


def on_device(dp_n, groups, img_feat, txt_feat, img_weight, txt_weight, log_temp, bias):
    arrays = (img_feat, txt_feat, img_weight, txt_weight, log_temp, bias)
    rows = img_feat.shape[0]
    wide, embed = img_weight.shape
    depth_n = dp_n // SIDE
    held = embed * rows * (12 * SIDE * groups + 10 * depth_n + 28 * groups)
    held += 2 * rows * dp_n * groups * (wide + embed // depth_n) + 12 * wide * embed
    if (
        dp_n % SIDE or groups != 4 or rows % 16 or wide % 128 or wide % (16 * CHUNKS)
        or embed % 256
        or embed % (128 * depth_n) or held > 40 * 2**20
    ):
        return by_collectives(*arrays)
    return in_one_kernel(dp_n, groups, *arrays)


def solution(mesh):
    placed = (
        P(("dp", "fsdp"), None),
        P(("dp", "fsdp"), None),
        P("fsdp", None),
        P("fsdp", None),
        P(),
        P(),
    )
    return jax.shard_map(
        functools.partial(on_device, mesh.shape["dp"], mesh.shape["fsdp"]),
        mesh=mesh,
        in_specs=placed,
        out_specs=(P("fsdp", None), P("fsdp", None)),
        check_vma=False,
    )
```
